512 devices in a mesh: ctx: 64 (over z, x_hi, core), tp: 8 (over x_lo, y).
Axes of the slice: x: 4 (x_hi: 2, x_lo: 2; x = x_hi * 2 + x_lo), y: 4, z: 16, core: 2. Of those that a mesh axis runs over, the one named last changes fastest.
Arguments:
- queries: bfloat16 [8192, 8192], P('ctx', 'tp'), may hold values from -34 to 34
- keys_values: bfloat16 [8192, 1024], P('ctx', 'tp'), may hold values from -34 to 34
- block_order: int32 [64], replicated, may hold values from 0 to 63, each once
- tokens: bfloat16 [4096, 4096], P('ctx', 'tp'), may hold values from -6 to 6
- route_ids: int32 [4096, 8], P('ctx'), may hold values from 0 to 63, all different within a row; in each aligned block of 64 rows (0 to 63, 64 to 127, ...) at most 9 rows name the same one
- route_gates: float32 [4096, 8], P('ctx'), may hold values from 0.05 to 0.3
- w_gate: bfloat16 [64, 4096, 1024], P('ctx', None, 'tp'), may hold values from -0.09375 to 0.09375
- w_up: bfloat16 [64, 4096, 1024], P('ctx', None, 'tp'), may hold values from -0.09375 to 0.09375
- w_down: bfloat16 [64, 1024, 4096], P('ctx', None, 'tp'), may hold values from -0.1875 to 0.1875
Outputs:
- attended: bfloat16 [8192, 8192], P('ctx', 'tp')
- mixed: bfloat16 [4096, 4096], P('ctx', 'tp')
The draws below stay inside these ranges and needn't reach their ends.
Inputs may be any that keep to these rules, and one draw needn't show every extreme that they name: `block_order`: each ctx index holds a different sequence block. `route_ids`: each row names 8 different experts; within the rows of one ctx index (aligned blocks of 64 rows) no expert is named more than 9 times, a bound that some block reaches.
All inputs are finite; a program needn't handle non-finite values.
Results may differ from the reference program's by a relative error of at most 0.0057.
Values may be sent and summed in bfloat16 or wider, within the bound.
A program may use at most 64 MiB of HBM per device.

```python
import math
import jax
import jax.numpy as jnp
import numpy as np
from jax import lax

HQ = 64
KVH = 4
HD = 128
D = 4096
FF = 1024
EXPERTS = 64
TOPK = 8
STEPS = 4
TOK_A = 128
TOK_B = 64
TOKENS_A = 8192
TOKENS_B = 4096
CAP = 9
N_CTX = 64


def draw_queries(key, part):
    key = jax.random.fold_in(key, 11)
    drawn_key = jax.random.fold_in(key, 0)
    drawn = jnp.clip(jax.random.normal(drawn_key, (TOKENS_A, HQ * HD)), -4.0, 4.0)
    return drawn.astype(jnp.bfloat16)


def draw_keys_values(key, part):
    key = jax.random.fold_in(key, 23)
    drawn_key = jax.random.fold_in(key, 0)
    drawn = jnp.clip(jax.random.normal(drawn_key, (TOKENS_A, 2 * KVH * HD)), -4.0, 4.0)
    return drawn.astype(jnp.bfloat16)


def levels(own_key, extent, shards, low, largest):
    gain = 1.0
    for axis_at, parts in shards:
        steps = jax.random.uniform(jax.random.fold_in(jax.random.fold_in(own_key, 6), axis_at), (parts,), jnp.float32, low / len(shards), largest / len(shards))
        gain = gain * jnp.repeat(jnp.exp(steps), extent[axis_at] // parts).reshape((-1,) + (1,) * (len(extent) - 1 - axis_at))
    return gain


def deal_out(stream_key, own, number, rows, amount, top, bound, slope):
    ranking = jax.random.permutation(stream_key, amount)
    crowded, usual = portions_of(amount, rows * top, bound, slope, True), portions_of(amount, rows * top, bound, slope, False)
    places = jnp.arange(amount)

    def named(sizes, turn):
        used = int((sizes > 0).sum())
        fixed = max(1, used // 4)
        shifted = fixed + (places - fixed + turn * (used - fixed)) % max(1, amount - fixed)
        return jnp.zeros((amount,), jnp.int32).at[ranking[jnp.where(places < fixed, places, shifted)]].set(jnp.asarray(sizes, jnp.int32))

    sizes = jnp.where(number % 4 == 0, named(crowded, number // 4), named(usual, number - number // 4 - 1))
    mixed = jax.random.permutation(jax.random.fold_in(own, 3), amount)
    donor, taker = mixed[0:amount // 2 * 2:2], mixed[1:amount // 2 * 2:2]
    room = jnp.minimum(sizes[donor] - 1, bound - sizes[taker]) // 2
    room = jnp.where((donor == ranking[0]) | (taker == ranking[0]) | (sizes[taker] == 0), 0, jnp.maximum(room, 0))
    shifted = jax.random.randint(jax.random.fold_in(own, 4), (amount // 2,), 0, 1 << 20) % (room + 1)
    sizes = sizes.at[donor].add(-shifted).at[taker].add(shifted)
    labels = jnp.searchsorted(jnp.cumsum(sizes), jnp.arange(rows * top), side="right").astype(jnp.int32)
    table = labels.reshape(top, rows).T
    table = table[jax.random.permutation(jax.random.fold_in(own, 1), rows)]
    turn = jax.random.randint(jax.random.fold_in(own, 2), (rows, 1), 0, top)
    return jnp.take_along_axis(table, (jnp.arange(top)[None, :] + turn) % top, axis=1)


def portions_of(amount, total, limit, slope, full):
    weights = [(1 << 20) // math.isqrt(standing ** slope) + 1 for standing in range(1, amount + 1)]
    largest = limit if full else min(limit, max(-(-total // amount), total * weights[0] // sum(weights)))
    least = 1 if total - largest >= amount - 1 else 0
    counts, surplus = [largest] + [least] * (amount - 1), total - largest - least * (amount - 1)
    while surplus > 0:
        free = [i for i in range(1, amount) if counts[i] < largest] or [i for i in range(1, amount) if counts[i] < limit]
        mass, left = sum([weights[i] for i in free]), surplus
        for i in free:
            more = min(limit - counts[i], max(1, left * weights[i] // mass), surplus)
            counts[i] = counts[i] + more
            surplus = surplus - more
    return np.array(counts)


def normal_values(key, dims, scale, reach, shards=(), kind=jnp.bfloat16):
    result = jax.random.normal(key, dims, jnp.float32) * scale
    if len(shards) > 0:
        result = levels(key, dims, shards, -0.22, 0.18) * result
    return jnp.clip(result, min=-reach, max=reach).astype(kind)


def setup_inputs(seed: int = 0) -> dict:
    keys = jax.random.split(jax.random.key(seed), 10)
    queries = draw_queries(jax.random.fold_in(keys[9], 71), 0)
    keys_values = draw_keys_values(jax.random.fold_in(keys[9], 71), 0)
    block_order = jax.random.permutation(keys[2], N_CTX).astype(jnp.int32)
    tokens = normal_values(keys[3], (TOKENS_B, D), 1.0, 6.0, ((0, 64), (1, 8)))
    route_ids_keys = jax.random.split(jax.random.fold_in(keys[4], 1), TOKENS_B // TOK_B)
    route_ids_turns = jax.random.permutation(jax.random.fold_in(keys[4], 3), TOKENS_B // TOK_B)
    route_ids = jax.vmap(lambda own, number: deal_out(jax.random.fold_in(keys[4], 2), own, number, TOK_B, EXPERTS, TOPK, CAP, 2))(route_ids_keys, route_ids_turns).reshape((TOKENS_B, TOPK))
    route_gates = jnp.clip(0.05 + 0.25 * jax.random.uniform(keys[5], (TOKENS_B, TOPK), jnp.float32) ** levels(keys[5], (TOKENS_B, TOPK), ((0, 64),), -0.2, 0.2), 0.05, 0.3)
    w_gate = normal_values(keys[6], (EXPERTS, D, FF), D ** -0.5, 0.09375, ((0, 64), (2, 8)))
    w_up = normal_values(keys[7], (EXPERTS, D, FF), D ** -0.5, 0.09375, ((0, 64), (2, 8)))
    w_down = normal_values(keys[8], (EXPERTS, FF, D), FF ** -0.5, 0.1875, ((0, 64), (2, 8)))
    return {"queries": queries, "keys_values": keys_values, "block_order": block_order, "tokens": tokens, "route_ids": route_ids, "route_gates": route_gates, "w_gate": w_gate, "w_up": w_up, "w_down": w_down}


masked_score = -1e+30

def attend_owner(owner, queries, keys_values, block_order):
    query_heads = lax.dynamic_slice_in_dim(queries, owner * TOK_A, TOK_A, 0)
    query_heads = query_heads.astype(jnp.float32).reshape(TOK_A, KVH, HQ // KVH, HD)
    sources = (owner - jnp.arange(STEPS, dtype=jnp.int32)) % N_CTX
    stacked = jnp.concatenate([lax.dynamic_slice_in_dim(keys_values, sources[cycle_step] * TOK_A, TOK_A, 0) for cycle_step in range(STEPS)], axis=0)
    stacked = stacked.astype(jnp.float32).reshape(STEPS * TOK_A, 2, KVH, HD)
    key_heads = stacked[:, 0]
    value_heads = stacked[:, 1]
    scores = jnp.einsum('qkgd,ckd->kgqc', query_heads, key_heads) / math.sqrt(HD)
    offsets = jnp.arange(TOK_A, dtype=jnp.int32)
    query_place = block_order[owner] * TOK_A + offsets
    key_place = (block_order[sources][:, None] * TOK_A + offsets[None, :]).reshape(STEPS * TOK_A)
    visible = key_place[None, :] <= query_place[:, None]
    scores = jnp.where(visible, scores, masked_score)
    row_peak = lax.optimization_barrier(jnp.max(scores, axis=-1, keepdims=True))
    weights = jnp.exp(scores - row_peak)
    weight_total = lax.optimization_barrier(jnp.sum(weights, axis=-1, keepdims=True))
    rounded = lax.optimization_barrier(weights.astype(jnp.bfloat16)).astype(jnp.float32)
    blended = jnp.einsum('kgqc,ckd->kgqd', rounded, value_heads) / weight_total
    return jnp.transpose(blended, (2, 0, 1, 3)).reshape(TOK_A, HQ * HD).astype(jnp.bfloat16)

def mixture(tokens, route_ids, route_gates, w_gate, w_up, w_down):
    entry_ids = route_ids.reshape(N_CTX, TOK_B * TOPK)
    entry_gates = route_gates.reshape(N_CTX, TOK_B * TOPK)
    expert_iota = jnp.arange(EXPERTS, dtype=jnp.int32)
    onehot = (entry_ids[:, :, None] == expert_iota[None, None, :]).astype(jnp.int32)
    slot_rank = lax.optimization_barrier(jnp.sum((jnp.cumsum(onehot, axis=1) - 1) * onehot, axis=2))
    slot_index = entry_ids * CAP + slot_rank
    entry_token = jnp.broadcast_to((jnp.arange(TOK_B * TOPK, dtype=jnp.int32) // TOPK)[None, :], (N_CTX, TOK_B * TOPK))
    block_iota = jnp.arange(N_CTX, dtype=jnp.int32)
    slot_table = jnp.full((N_CTX, EXPERTS * CAP), TOK_B, jnp.int32)
    slot_table = slot_table.at[block_iota[:, None], slot_index].set(entry_token)
    gate_table = jnp.zeros((N_CTX, EXPERTS * CAP), jnp.float32)
    gate_table = gate_table.at[block_iota[:, None], slot_index].set(entry_gates)
    blocks = tokens.reshape(N_CTX, TOK_B, D)
    padded = jnp.concatenate([blocks, jnp.zeros((N_CTX, 1, D), jnp.bfloat16)], axis=1)

    def one_expert(carried, expert):
        chosen = lax.dynamic_slice_in_dim(slot_table, expert * CAP, CAP, 1)
        slot_gates = lax.dynamic_slice_in_dim(gate_table, expert * CAP, CAP, 1)
        gathered = jnp.take_along_axis(padded, chosen[:, :, None], axis=1).reshape(N_CTX * CAP, D)
        gate_sum = jnp.dot(gathered, w_gate[expert], preferred_element_type=jnp.float32)
        up_sum = jnp.dot(gathered, w_up[expert], preferred_element_type=jnp.float32)
        hidden = (jax.nn.silu(gate_sum) * up_sum).astype(jnp.bfloat16)
        expert_out = jnp.dot(hidden, w_down[expert], preferred_element_type=jnp.float32)
        expert_out = expert_out.astype(jnp.bfloat16).astype(jnp.float32).reshape(N_CTX, CAP, D)
        carried = carried.at[block_iota[:, None], chosen].add(slot_gates[:, :, None] * expert_out)
        return (carried, None)
    initial = jnp.zeros((N_CTX, TOK_B + 1, D), jnp.float32)
    summed, unused = lax.scan(one_expert, initial, expert_iota)
    return summed[:, :TOK_B].reshape(N_CTX * TOK_B, D).astype(jnp.bfloat16)

def reference(queries, keys_values, block_order, tokens, route_ids, route_gates, w_gate, w_up, w_down):
    owners = jnp.arange(N_CTX, dtype=jnp.int32)
    attended = lax.map(lambda owner: attend_owner(owner, queries, keys_values, block_order), owners)
    attended = attended.reshape(N_CTX * TOK_A, HQ * HD)
    mixed = mixture(tokens, route_ids, route_gates, w_gate, w_up, w_down)
    return (attended, mixed)
```

```python
import math

import jax
import jax.numpy as jnp
from jax import lax
from jax.experimental import pallas as pl
from jax.experimental.pallas import tpu as pltpu
from jax.sharding import PartitionSpec as P

HD = 128
EXPERTS = 64
TOPK = 8
STEPS = 4
CAP = 9
Z = 16
NEAR = 4
Y = 4
TP = 8
TOK = 64
QROWS = 128
HEADS = 8
WIDE = 512
LANES = 128
COLS = WIDE // LANES
FF = 128

OFFSETS = (0, 1, 15, 2, 14, 3, 13, 4, 12, 5, 11, 6, 10, 7, 9, 8)
GROUPS = 4
PER = 16
ROWS = PER * CAP
FLAT = ROWS * COLS

MASKED = -1e30
f32 = jnp.float32
bf16 = jnp.bfloat16
i32 = jnp.int32


def dot(a, b):
    return jnp.dot(a, b, preferred_element_type=f32)


def iota(shape, dim):
    return lax.broadcasted_iota(i32, shape, dim)


def kernel(
    queries, keys_values, block_order, tokens, ids, gates, w_gate, w_up, w_down,
    attended, mixed,
    outgoing, arriving, rows_all, hidden_all, going_back, returned, kv_all, q_here, w_in, w_out,
    dispatch, gate_high, gate_low, perm_in, perm_out, total,
    load_sem, out_send, out_recv, back_send, back_recv, row_send, row_recv, hid_send, hid_recv,
    kv_send, kv_recv,
):
    ctx = lax.axis_index("ctx")
    tp = lax.axis_index("tp")
    n_ctx = Z * NEAR
    z, near = ctx // NEAR, ctx % NEAR
    x_lo, y = tp // Y, tp % Y
    barrier = pltpu.get_barrier_semaphore()

    def at(c, t):
        return {"ctx": c, "tp": t}

    def greet(c, t):
        pl.semaphore_signal(barrier, inc=1, device_id=at(c, t), device_id_type=pl.DeviceIdType.MESH)

    def send(src, dst, send_sem, recv_sem, c, t):
        copy = pltpu.make_async_remote_copy(
            src_ref=src, dst_ref=dst, send_sem=send_sem, recv_sem=recv_sem,
            device_id=at(c, t), device_id_type=pl.DeviceIdType.MESH,
        )
        copy.start()

    def wait(ref, sem):
        pltpu.make_async_copy(ref, ref, sem).wait()

    def greet_ctx(i, carry):
        greet((ctx + i) % n_ctx, tp)
        return carry

    def greet_tp(i, carry):
        greet(ctx, (tp + i) % TP)
        return carry

    lax.fori_loop(1, n_ctx, greet_ctx, 0)
    lax.fori_loop(1, TP, greet_tp, 0)
    own_kv = (tp == 0) | (tp == TP - 1)
    kv_from = [(s, kind) for s in range(STEPS) for kind in range(2)]
    for s, kind in kv_from:
        if s == 0:
            @pl.when(4 * kind + tp // 2 != tp)
            def _():
                greet(ctx, 4 * kind + tp // 2)
        else:
            greet((ctx + n_ctx - s) % n_ctx, 4 * kind + tp // 2)

    loads = [
        pltpu.make_async_copy(w_gate.at[0], w_in.at[:, pl.ds(0, FF)], load_sem.at[0]),
        pltpu.make_async_copy(w_up.at[0], w_in.at[:, pl.ds(FF, FF)], load_sem.at[1]),
        pltpu.make_async_copy(w_down.at[0], w_out, load_sem.at[2]),
        pltpu.make_async_copy(queries, q_here, load_sem.at[3]),
    ]
    for load in loads:
        load.start()

    place = iota((EXPERTS, TOK), 0)
    turn = lax.shift_right_logical(place, 2)
    offset = jnp.zeros((EXPERTS, TOK), i32)
    for i, o in enumerate(OFFSETS):
        offset = jnp.where(turn == i, o, offset)
    expert = ((z + offset) & (Z - 1)) * NEAR + (place & (NEAR - 1))
    named = jnp.zeros((EXPERTS, TOK), f32)
    gate_of = jnp.zeros((EXPERTS, TOK), f32)
    for k in range(TOPK):
        hit = ids[pl.ds(k, 1), :] == expert
        named = jnp.where(hit, 1.0, named)
        gate_of = jnp.where(hit, gates[pl.ds(k, 1), :], gate_of)
    earlier = (iota((TOK, TOK), 0) < iota((TOK, TOK), 1)).astype(f32).astype(bf16)
    rank = dot(named.astype(bf16), earlier)
    coded = jnp.concatenate(
        [jnp.where(named > 0, rank + 16.0 * j, -1.0) for j in range(COLS)], axis=1
    ).astype(bf16)
    gate4 = jnp.concatenate([gate_of] * COLS, axis=1)
    gate4_high = gate4.astype(bf16)
    gate4_low = (gate4 - gate4_high.astype(f32)).astype(bf16)

    line = iota((FLAT, LANES), 0).astype(f32)
    block = jnp.floor((line + 0.5) * (1.0 / (CAP * COLS)))
    within = line - block * (CAP * COLS)
    slot = jnp.floor((within + 0.5) * (1.0 / COLS))
    code = slot + 16.0 * (within - slot * COLS)
    spread = (block[:, :PER] == iota((FLAT, PER), 1).astype(f32)).astype(f32).astype(bf16)
    token_cols = jnp.concatenate(
        [tokens[:, pl.ds(j * LANES, LANES)] for j in range(COLS)], axis=0
    )

    def fill(g):
        codes = dot(spread, coded[g * PER:(g + 1) * PER])
        chosen = jnp.concatenate(
            [(codes[:, :LANES] == code).astype(f32), (codes[:, LANES:] == code).astype(f32)], axis=1
        ).astype(bf16)
        dispatch[g] = chosen
        outgoing[pl.ds(g * PER, PER)] = (
            dot(chosen, token_cols).astype(bf16).reshape(PER, CAP, COLS, LANES)
        )

    for g in range(GROUPS):
        fill(g)

    to = iota((FLAT, FLAT), 1).astype(f32)
    at_row = iota((FLAT, FLAT), 0).astype(f32)
    col = jnp.floor((at_row + 0.5) * (1.0 / ROWS))
    perm_in[...] = (to == COLS * (at_row - ROWS * col) + col).astype(f32).astype(bf16)
    row = jnp.floor((at_row + 0.5) * (1.0 / COLS))
    perm_out[...] = (to == ROWS * (at_row - COLS * row) + row).astype(f32).astype(bf16)

    pl.semaphore_wait(barrier, (n_ctx - 1) + (TP - 1) + 2 * STEPS - own_kv.astype(i32))

    def scatter_blocks(src, dst, send_sems, recv_sems, g, way):
        for i in range(4):
            o = OFFSETS[g * 4 + i]
            base = (g * 4 + i) * NEAR
            far = (z + way * o + Z) % Z
            for d in range(NEAR):
                if o == 0 and d == 0:
                    pltpu.make_async_copy(
                        src.at[base + near], dst.at[base + near], recv_sems.at[g]
                    ).start()
                    continue
                there = (near + d) % NEAR
                send(
                    src.at[base + there], dst.at[base + near], send_sems.at[g], recv_sems.at[g],
                    far * NEAR + there, tp,
                )

    for g in range(GROUPS):
        scatter_blocks(outgoing, arriving, out_send, out_recv, g, 1)

    kind_here = tp // 4
    for s in range(STEPS):
        for d in range(2):
            target = 2 * (tp % 4) + d
            dst = kv_all.at[kind_here, pl.ds(s * QROWS, QROWS)]
            sem = kv_send.at[2 * s + d]
            if s > 0:
                send(keys_values, dst, sem, kv_recv, (ctx + s) % n_ctx, target)
            else:
                @pl.when(target != tp)
                def _():
                    send(keys_values, dst, sem, kv_recv, ctx, target)

                @pl.when(target == tp)
                def _():
                    pltpu.make_async_copy(keys_values, dst, kv_recv).start()

    for g in range(GROUPS):
        high = dot(spread, gate4_high[g * PER:(g + 1) * PER])
        low = dot(spread, gate4_low[g * PER:(g + 1) * PER])
        chosen = dispatch[g].astype(f32)
        gate_high[g] = (chosen * high).T.astype(bf16)
        gate_low[g] = (chosen * low).T.astype(bf16)

    up_y, down_y = (y + 1) % Y, (y + Y - 1) % Y
    partner = (1 - x_lo) * Y + y
    up_tp, down_tp = x_lo * Y + up_y, x_lo * Y + down_y

    def take_rows(g):
        wait(arriving.at[pl.ds(g * PER, PER)], out_recv.at[g])
        flat = arriving[pl.ds(g * PER, PER)].reshape(FLAT, LANES)
        sorted_rows = dot(perm_in[...], flat).astype(bf16)
        for j in range(COLS):
            rows_all[g, y, x_lo, :, pl.ds(j * LANES, LANES)] = sorted_rows[j * ROWS:(j + 1) * ROWS]
        mine = rows_all.at[g, y, x_lo]
        send(mine, mine, row_send.at[g, 0], row_recv.at[g, 0], ctx, partner)

    def pass_y(g):
        wait(rows_all.at[g, y, 1 - x_lo], row_recv.at[g, 0])
        both = rows_all.at[g, y]
        send(both, both, row_send.at[g, 1], row_recv.at[g, 1], ctx, up_tp)
        send(both, both, row_send.at[g, 2], row_recv.at[g, 2], ctx, down_tp)

    def pass_on(g):
        wait(rows_all.at[g, down_y], row_recv.at[g, 1])
        below = rows_all.at[g, down_y, 0]
        send(below, below, row_send.at[g, 3], row_recv.at[g, 3], ctx, up_tp)
        wait(rows_all.at[g, up_y], row_recv.at[g, 2])
        above = rows_all.at[g, up_y, 1]
        send(above, above, row_send.at[g, 4], row_recv.at[g, 4], ctx, down_tp)

    def first_half(g):
        if g == 0:
            loads[0].wait()
            loads[1].wait()
        wait(rows_all.at[g, 0, 0], row_recv.at[g, 3])
        wait(rows_all.at[g, 0, 0], row_recv.at[g, 4])
        sums = jnp.zeros((ROWS, 2 * FF), f32)
        for xx in range(2):
            for yy in range(Y):
                sums += dot(
                    rows_all[g, yy, xx], w_in[pl.ds((xx * Y + yy) * WIDE, WIDE), :]
                )
        gate_sum, up_sum = sums[:, :FF], sums[:, FF:]
        hidden = gate_sum / (1.0 + jnp.exp(-gate_sum)) * up_sum
        hidden_all[g, tp] = hidden.astype(bf16)
        mine = hidden_all.at[g, tp]
        for i in range(1, TP):
            send(mine, mine, hid_send.at[g], hid_recv.at[g], ctx, (tp + i) % TP)

    def second_half(g):
        if g == 0:
            loads[2].wait()
        wait(hidden_all.at[g, pl.ds(0, TP - 1)], hid_recv.at[g])
        sums = jnp.zeros((ROWS, WIDE), f32)
        for t in range(TP):
            sums += dot(hidden_all[g, t], w_out[pl.ds(t * FF, FF), :])
        out = sums.astype(bf16)
        stacked = jnp.concatenate([out[:, j * LANES:(j + 1) * LANES] for j in range(COLS)], axis=0)
        going_back[pl.ds(g * PER, PER)] = (
            dot(perm_out[...], stacked).astype(bf16).reshape(PER, CAP, COLS, LANES)
        )
        scatter_blocks(going_back, returned, back_send, back_recv, g, -1)

    def mix(g):
        wait(returned.at[pl.ds(g * PER, PER)], back_recv.at[g])
        flat = returned[pl.ds(g * PER, PER)].reshape(FLAT, LANES)
        part = dot(gate_high[g], flat) + dot(gate_low[g], flat)
        if g == 0:
            total[...] = part
        else:
            total[...] += part

    own_block = block_order[ctx]

    def attend(first, last):
        if first == 0:
            loads[3].wait()
            wait(kv_all, kv_recv)
        query_place = own_block * QROWS + iota((QROWS, QROWS), 0)
        key_offset = iota((QROWS, QROWS), 1)
        visible = jnp.concatenate(
            [
                jnp.where(
                    block_order[(ctx + n_ctx - s) % n_ctx] * QROWS + key_offset <= query_place, 1.0, 0.0
                )
                for s in range(STEPS)
            ],
            axis=1,
        )
        for h in range(first, last):
            scores = lax.dot_general(
                q_here[:, pl.ds(h * HD, HD)], kv_all[0], (((1,), (1,)), ((), ())),
                preferred_element_type=f32,
            ) * (1.0 / math.sqrt(HD))
            scores = jnp.where(visible > 0.5, scores, MASKED)
            weights = jnp.exp(scores - jnp.max(scores, axis=1, keepdims=True))
            weight_total = jnp.sum(weights, axis=1, keepdims=True)
            blended = dot(weights.astype(bf16), kv_all[1]) / weight_total
            attended[:, pl.ds(h * HD, HD)] = blended.astype(bf16)

    take_rows(0)
    pass_y(0)
    take_rows(1)
    pass_on(0)
    pass_y(1)
    attend(0, 4)
    take_rows(2)
    first_half(0)
    pass_on(1)
    pass_y(2)
    take_rows(3)
    attend(4, 8)
    second_half(0)
    first_half(1)
    pass_on(2)
    pass_y(3)
    second_half(1)
    first_half(2)
    pass_on(3)
    second_half(2)
    mix(0)
    first_half(3)
    second_half(3)
    mix(1)
    mix(2)
    mix(3)
    for j in range(COLS):
        mixed[:, pl.ds(j * LANES, LANES)] = total[pl.ds(j * TOK, TOK), :].astype(bf16)

    for g in range(GROUPS):
        count = PER - 1 if 0 in OFFSETS[g * 4:g * 4 + 4] else PER
        wait(outgoing.at[pl.ds(g * PER, count)], out_send.at[g])
        wait(going_back.at[pl.ds(g * PER, count)], back_send.at[g])
        wait(rows_all.at[g, 0, 0], row_send.at[g, 0])
        wait(rows_all.at[g, 0], row_send.at[g, 1])
        wait(rows_all.at[g, 0], row_send.at[g, 2])
        wait(rows_all.at[g, 0, 0], row_send.at[g, 3])
        wait(rows_all.at[g, 0, 0], row_send.at[g, 4])
        wait(hidden_all.at[g, pl.ds(0, TP - 1)], hid_send.at[g])
    for s in range(STEPS):
        for d in range(2):
            if s > 0:
                wait(keys_values, kv_send.at[2 * s + d])
            else:
                @pl.when(2 * (tp % 4) + d != tp)
                def _():
                    wait(keys_values, kv_send.at[2 * s + d])


def shards(queries, keys_values, block_order, tokens, route_ids, route_gates, w_gate, w_up, w_down):
    vmem = pl.BlockSpec(memory_space=pltpu.VMEM)
    smem = pl.BlockSpec(memory_space=pltpu.SMEM)
    anywhere = pl.BlockSpec(memory_space=pl.ANY)
    dma = pltpu.SemaphoreType.DMA
    blocks = (GROUPS * PER, CAP, COLS, LANES)
    return pl.pallas_call(
        kernel,
        out_shape=(
            jax.ShapeDtypeStruct((QROWS, HEADS * HD), bf16),
            jax.ShapeDtypeStruct((TOK, WIDE), bf16),
        ),
        in_specs=[anywhere, vmem, smem, vmem, vmem, vmem, anywhere, anywhere, anywhere],
        out_specs=(vmem, vmem),
        scratch_shapes=[
            pltpu.VMEM(blocks, bf16),
            pltpu.VMEM(blocks, bf16),
            pltpu.VMEM((GROUPS, Y, 2, ROWS, WIDE), bf16),
            pltpu.VMEM((GROUPS, TP, ROWS, FF), bf16),
            pltpu.VMEM(blocks, bf16),
            pltpu.VMEM(blocks, bf16),
            pltpu.VMEM((2, STEPS * QROWS, HD), bf16),
            pltpu.VMEM((QROWS, HEADS * HD), bf16),
            pltpu.VMEM((TP * WIDE, 2 * FF), bf16),
            pltpu.VMEM((TP * FF, WIDE), bf16),
            pltpu.VMEM((GROUPS, FLAT, COLS * TOK), bf16),
            pltpu.VMEM((GROUPS, COLS * TOK, FLAT), bf16),
            pltpu.VMEM((GROUPS, COLS * TOK, FLAT), bf16),
            pltpu.VMEM((FLAT, FLAT), bf16),
            pltpu.VMEM((FLAT, FLAT), bf16),
            pltpu.VMEM((COLS * TOK, LANES), f32),
            dma((4,)),
            dma((GROUPS,)),
            dma((GROUPS,)),
            dma((GROUPS,)),
            dma((GROUPS,)),
            dma((GROUPS, 5)),
            dma((GROUPS, 5)),
            dma((GROUPS,)),
            dma((GROUPS,)),
            dma((2 * STEPS,)),
            dma,
        ],
        compiler_params=pltpu.CompilerParams(
            collective_id=0, has_side_effects=True, vmem_limit_bytes=48 * 1024 * 1024
        ),
    )(queries, keys_values, block_order, tokens, route_ids.T, route_gates.T, w_gate, w_up, w_down)


def solution(mesh):
    in_specs = (
        P("ctx", "tp"),
        P("ctx", "tp"),
        P(),
        P("ctx", "tp"),
        P("ctx", None),
        P("ctx", None),
        P("ctx", None, "tp"),
        P("ctx", None, "tp"),
        P("ctx", None, "tp"),
    )
    out_specs = (P("ctx", "tp"), P("ctx", "tp"))
    return jax.shard_map(shards, mesh=mesh, in_specs=in_specs, out_specs=out_specs, check_vma=False)
```

```python
import math

import jax
import jax.numpy as jnp
from jax import lax
from jax.experimental import pallas as pl
from jax.experimental.pallas import tpu as pltpu
from jax.sharding import PartitionSpec as P

HD = 128
EXPERTS = 64
TOPK = 8
STEPS = 4
CAP = 9
Z = 16
NEAR = 4
Y = 4
TP = 8
TOK = 64
QROWS = 128
HEADS = 8
WIDE = 512
LANES = 128
COLS = WIDE // LANES
FF = 128

OFFSETS = (0, 1, 15, 2, 3, 14, 8, 9, 4, 13, 7, 10, 5, 12, 6, 11)
GROUPS = 4
PER = 16
ROWS = PER * CAP
FLAT = ROWS * COLS

MASKED = -1e30
f32 = jnp.float32
bf16 = jnp.bfloat16
i32 = jnp.int32


def dot(a, b):
    return jnp.dot(a, b, preferred_element_type=f32)


def iota(shape, dim):
    return lax.broadcasted_iota(i32, shape, dim)


def kernel(
    queries, keys_values, block_order, tokens, ids, gates, w_gate, w_up, w_down,
    attended, mixed,
    outgoing, arriving, rows_all, hidden_all, going_back, returned, kv_all, q_here, w_in, w_out,
    dispatch, gate_high, gate_low, perm_in, perm_out, total,
    load_sem, out_send, out_recv, back_send, back_recv, row_send, row_recv, hid_send, hid_recv,
    kv_send, kv_recv, near_sem,
):
    ctx = lax.axis_index("ctx")
    tp = lax.axis_index("tp")
    n_ctx = Z * NEAR
    z, near = ctx // NEAR, ctx % NEAR
    x_lo, y = tp // Y, tp % Y
    barrier = pltpu.get_barrier_semaphore()

    def at(c, t):
        return {"ctx": c, "tp": t}

    def greet(c, t):
        pl.semaphore_signal(barrier, inc=1, device_id=at(c, t), device_id_type=pl.DeviceIdType.MESH)

    def send(src, dst, send_sem, recv_sem, c, t):
        copy = pltpu.make_async_remote_copy(
            src_ref=src, dst_ref=dst, send_sem=send_sem, recv_sem=recv_sem,
            device_id=at(c, t), device_id_type=pl.DeviceIdType.MESH,
        )
        copy.start()

    def wait(ref, sem):
        pltpu.make_async_copy(ref, ref, sem).wait()

    up_y, down_y = (y + 1) % Y, (y + Y - 1) % Y
    partner = (1 - x_lo) * Y + y
    up_tp, down_tp = x_lo * Y + up_y, x_lo * Y + down_y

    def greet_z(i, carry):
        greet((z + i) % Z * NEAR + near, tp)
        return carry

    lax.fori_loop(1, Z, greet_z, 0)
    for i in range(1, NEAR):
        greet(z * NEAR + (near + i) % NEAR, tp)
    for t in (partner, up_tp, down_tp):
        greet(ctx, t)
    own_kv = (tp == 0) | (tp == TP - 1)
    for kind in range(2):
        @pl.when(4 * kind + tp // 2 != tp)
        def _():
            greet(ctx, 4 * kind + tp // 2)

    loads = [
        pltpu.make_async_copy(w_gate.at[0], w_in.at[:, pl.ds(0, FF)], load_sem.at[0]),
        pltpu.make_async_copy(w_up.at[0], w_in.at[:, pl.ds(FF, FF)], load_sem.at[1]),
        pltpu.make_async_copy(w_down.at[0], w_out, load_sem.at[2]),
        pltpu.make_async_copy(queries, q_here, load_sem.at[3]),
    ]
    for load in loads:
        load.start()

    place = iota((EXPERTS, TOK), 0)
    turn = lax.shift_right_logical(place, 2)
    offset = jnp.zeros((EXPERTS, TOK), i32)
    for i, o in enumerate(OFFSETS):
        offset = jnp.where(turn == i, o, offset)
    expert = ((z + offset) & (Z - 1)) * NEAR + (place & (NEAR - 1))
    named = jnp.zeros((EXPERTS, TOK), f32)
    gate_of = jnp.zeros((EXPERTS, TOK), f32)
    for k in range(TOPK):
        hit = ids[pl.ds(k, 1), :] == expert
        named = jnp.where(hit, 1.0, named)
        gate_of = jnp.where(hit, gates[pl.ds(k, 1), :], gate_of)
    earlier = (iota((TOK, TOK), 0) < iota((TOK, TOK), 1)).astype(f32).astype(bf16)
    rank = dot(named.astype(bf16), earlier)
    coded = jnp.concatenate(
        [jnp.where(named > 0, rank + 16.0 * j, -1.0) for j in range(COLS)], axis=1
    ).astype(bf16)
    gate4 = jnp.concatenate([gate_of] * COLS, axis=1)
    gate4_high = gate4.astype(bf16)
    gate4_low = (gate4 - gate4_high.astype(f32)).astype(bf16)

    line = iota((FLAT, LANES), 0).astype(f32)
    block = jnp.floor((line + 0.5) * (1.0 / (CAP * COLS)))
    within = line - block * (CAP * COLS)
    slot = jnp.floor((within + 0.5) * (1.0 / COLS))
    code = slot + 16.0 * (within - slot * COLS)
    spread = (block[:, :PER] == iota((FLAT, PER), 1).astype(f32)).astype(f32).astype(bf16)
    token_cols = jnp.concatenate(
        [tokens[:, pl.ds(j * LANES, LANES)] for j in range(COLS)], axis=0
    )

    def fill(g):
        codes = dot(spread, coded[g * PER:(g + 1) * PER])
        chosen = jnp.concatenate(
            [(codes[:, :LANES] == code).astype(f32), (codes[:, LANES:] == code).astype(f32)], axis=1
        ).astype(bf16)
        dispatch[g] = chosen
        outgoing[pl.ds(g * PER, PER)] = (
            dot(chosen, token_cols).astype(bf16).reshape(PER, CAP, COLS, LANES)
        )

    for g in range(GROUPS):
        fill(g)

    to = iota((FLAT, FLAT), 1).astype(f32)
    at_row = iota((FLAT, FLAT), 0).astype(f32)
    col = jnp.floor((at_row + 0.5) * (1.0 / ROWS))
    perm_in[...] = (to == COLS * (at_row - ROWS * col) + col).astype(f32).astype(bf16)
    row = jnp.floor((at_row + 0.5) * (1.0 / COLS))
    perm_out[...] = (to == ROWS * (at_row - COLS * row) + row).astype(f32).astype(bf16)

    pl.semaphore_wait(barrier, (Z - 1) + (NEAR - 1) + 3 + 2 - own_kv.astype(i32))
    for i in range(1, NEAR):
        pl.semaphore_signal(
            near_sem, inc=1, device_id=at(z * NEAR + (near + i) % NEAR, tp), device_id_type=pl.DeviceIdType.MESH
        )
    pl.semaphore_wait(near_sem, NEAR - 1)

    def scatter_blocks(src, dst, send_sems, recv_sems, g, way):
        for i in range(4):
            o = OFFSETS[g * 4 + i]
            base = (g * 4 + i) * NEAR
            far = (z + way * o + Z) % Z
            for d in range(NEAR):
                if o == 0 and d == 0:
                    pltpu.make_async_copy(
                        src.at[base + near], dst.at[base + near], recv_sems.at[g]
                    ).start()
                    continue
                there = (near + d) % NEAR
                send(
                    src.at[base + there], dst.at[base + near], send_sems.at[g], recv_sems.at[g],
                    far * NEAR + there, tp,
                )

    for g in range(GROUPS):
        scatter_blocks(outgoing, arriving, out_send, out_recv, g, 1)

    for d in range(2):
        target = 2 * (tp % 4) + d
        dst = kv_all.at[0, tp // 4]

        @pl.when(target != tp)
        def _():
            send(keys_values, dst, kv_send.at[d], kv_recv.at[0], ctx, target)

        @pl.when(target == tp)
        def _():
            pltpu.make_async_copy(keys_values, dst, kv_recv.at[0]).start()

    def pass_kv(s):
        wait(kv_all.at[s - 1], kv_recv.at[s - 1])
        send(kv_all.at[s - 1], kv_all.at[s], kv_send.at[s + 1], kv_recv.at[s], (ctx + 1) % n_ctx, tp)

    for g in range(GROUPS):
        high = dot(spread, gate4_high[g * PER:(g + 1) * PER])
        low = dot(spread, gate4_low[g * PER:(g + 1) * PER])
        chosen = dispatch[g].astype(f32)
        gate_high[g] = (chosen * high).T.astype(bf16)
        gate_low[g] = (chosen * low).T.astype(bf16)

    def gather_x(parts, send_sem, recv_sem, g):
        mine = parts.at[g, y, x_lo]
        send(mine, mine, send_sem.at[g, 0], recv_sem.at[g, 0], ctx, partner)

    def gather_y(parts, send_sem, recv_sem, g):
        wait(parts.at[g, y, 1 - x_lo], recv_sem.at[g, 0])
        both = parts.at[g, y]
        send(both, both, send_sem.at[g, 1], recv_sem.at[g, 1], ctx, up_tp)
        send(both, both, send_sem.at[g, 2], recv_sem.at[g, 2], ctx, down_tp)

    def gather_on(parts, send_sem, recv_sem, g):
        wait(parts.at[g, down_y], recv_sem.at[g, 1])
        below = parts.at[g, down_y, 0]
        send(below, below, send_sem.at[g, 3], recv_sem.at[g, 3], ctx, up_tp)
        wait(parts.at[g, up_y], recv_sem.at[g, 2])
        above = parts.at[g, up_y, 1]
        send(above, above, send_sem.at[g, 4], recv_sem.at[g, 4], ctx, down_tp)

    def gather_end(parts, recv_sem, g):
        wait(parts.at[g, 0, 0], recv_sem.at[g, 3])
        wait(parts.at[g, 0, 0], recv_sem.at[g, 4])

    def gather_sent(parts, send_sem, g):
        for i, part in enumerate((parts.at[g, 0, 0], parts.at[g, 0], parts.at[g, 0], parts.at[g, 0, 0], parts.at[g, 0, 0])):
            wait(part, send_sem.at[g, i])

    def take_rows(g):
        wait(arriving.at[pl.ds(g * PER, PER)], out_recv.at[g])
        flat = arriving[pl.ds(g * PER, PER)].reshape(FLAT, LANES)
        sorted_rows = dot(perm_in[...], flat).astype(bf16)
        for j in range(COLS):
            rows_all[g, y, x_lo, :, pl.ds(j * LANES, LANES)] = sorted_rows[j * ROWS:(j + 1) * ROWS]
        gather_x(rows_all, row_send, row_recv, g)

    def pass_y(g):
        gather_y(rows_all, row_send, row_recv, g)

    def pass_on(g):
        gather_on(rows_all, row_send, row_recv, g)

    def hid_y(g):
        gather_y(hidden_all, hid_send, hid_recv, g)

    def hid_on(g):
        gather_on(hidden_all, hid_send, hid_recv, g)

    def first_half(g):
        if g == 0:
            loads[0].wait()
            loads[1].wait()
        gather_end(rows_all, row_recv, g)
        sums = jnp.zeros((ROWS, 2 * FF), f32)
        for xx in range(2):
            for yy in range(Y):
                sums += dot(
                    rows_all[g, yy, xx], w_in[pl.ds((xx * Y + yy) * WIDE, WIDE), :]
                )
        gate_sum, up_sum = sums[:, :FF], sums[:, FF:]
        hidden = gate_sum / (1.0 + jnp.exp(-gate_sum)) * up_sum
        hidden_all[g, y, x_lo] = hidden.astype(bf16)
        gather_x(hidden_all, hid_send, hid_recv, g)

    def second_half(g):
        if g == 0:
            loads[2].wait()
        gather_end(hidden_all, hid_recv, g)
        sums = jnp.zeros((ROWS, WIDE), f32)
        for xx in range(2):
            for yy in range(Y):
                sums += dot(hidden_all[g, yy, xx], w_out[pl.ds((xx * Y + yy) * FF, FF), :])
        out = sums.astype(bf16)
        stacked = jnp.concatenate([out[:, j * LANES:(j + 1) * LANES] for j in range(COLS)], axis=0)
        going_back[pl.ds(g * PER, PER)] = (
            dot(perm_out[...], stacked).astype(bf16).reshape(PER, CAP, COLS, LANES)
        )
        scatter_blocks(going_back, returned, back_send, back_recv, g, -1)

    def mix(g):
        wait(returned.at[pl.ds(g * PER, PER)], back_recv.at[g])
        flat = returned[pl.ds(g * PER, PER)].reshape(FLAT, LANES)
        part = dot(gate_high[g], flat) + dot(gate_low[g], flat)
        if g == 0:
            total[...] = part
        else:
            total[...] += part

    own_block = block_order[ctx]

    def attend(first, last):
        if first == 0:
            loads[3].wait()
            wait(kv_all.at[STEPS - 1], kv_recv.at[STEPS - 1])
        query_place = own_block * QROWS + iota((QROWS, QROWS), 0)
        key_offset = iota((QROWS, QROWS), 1)
        visible = jnp.concatenate(
            [
                jnp.where(
                    block_order[(ctx + n_ctx - s) % n_ctx] * QROWS + key_offset <= query_place, 1.0, 0.0
                )
                for s in range(STEPS)
            ],
            axis=1,
        )
        keys = jnp.concatenate([kv_all[s, 0] for s in range(STEPS)], axis=0)
        values = jnp.concatenate([kv_all[s, 1] for s in range(STEPS)], axis=0)
        for h in range(first, last):
            scores = lax.dot_general(
                q_here[:, pl.ds(h * HD, HD)], keys, (((1,), (1,)), ((), ())),
                preferred_element_type=f32,
            ) * (1.0 / math.sqrt(HD))
            scores = jnp.where(visible > 0.5, scores, MASKED)
            weights = jnp.exp(scores - jnp.max(scores, axis=1, keepdims=True))
            weight_total = jnp.sum(weights, axis=1, keepdims=True)
            blended = dot(weights.astype(bf16), values) / weight_total
            attended[:, pl.ds(h * HD, HD)] = blended.astype(bf16)

    take_rows(0)
    pass_y(0)
    pass_kv(1)
    take_rows(1)
    pass_kv(2)
    pass_on(0)
    pass_y(1)
    pass_kv(3)
    first_half(0)
    take_rows(2)
    hid_y(0)
    pass_on(1)
    pass_y(2)
    attend(0, 4)
    hid_on(0)
    first_half(1)
    take_rows(3)
    second_half(0)
    hid_y(1)
    pass_on(2)
    pass_y(3)
    attend(4, 8)
    hid_on(1)
    first_half(2)
    second_half(1)
    mix(0)
    hid_y(2)
    pass_on(3)
    hid_on(2)
    first_half(3)
    second_half(2)
    hid_y(3)
    mix(1)
    hid_on(3)
    second_half(3)
    mix(2)
    mix(3)
    for j in range(COLS):
        mixed[:, pl.ds(j * LANES, LANES)] = total[pl.ds(j * TOK, TOK), :].astype(bf16)

    for g in range(GROUPS):
        count = PER - 1 if 0 in OFFSETS[g * 4:g * 4 + 4] else PER
        wait(outgoing.at[pl.ds(g * PER, count)], out_send.at[g])
        wait(going_back.at[pl.ds(g * PER, count)], back_send.at[g])
        gather_sent(rows_all, row_send, g)
        gather_sent(hidden_all, hid_send, g)
    for d in range(2):
        @pl.when(2 * (tp % 4) + d != tp)
        def _():
            wait(keys_values, kv_send.at[d])
    for s in range(1, STEPS):
        wait(kv_all.at[s], kv_send.at[s + 1])


def shards(queries, keys_values, block_order, tokens, route_ids, route_gates, w_gate, w_up, w_down):
    vmem = pl.BlockSpec(memory_space=pltpu.VMEM)
    smem = pl.BlockSpec(memory_space=pltpu.SMEM)
    anywhere = pl.BlockSpec(memory_space=pl.ANY)
    dma = pltpu.SemaphoreType.DMA
    blocks = (GROUPS * PER, CAP, COLS, LANES)
    return pl.pallas_call(
        kernel,
        out_shape=(
            jax.ShapeDtypeStruct((QROWS, HEADS * HD), bf16),
            jax.ShapeDtypeStruct((TOK, WIDE), bf16),
        ),
        in_specs=[anywhere, vmem, smem, vmem, vmem, vmem, anywhere, anywhere, anywhere],
        out_specs=(vmem, vmem),
        scratch_shapes=[
            pltpu.VMEM(blocks, bf16),
            pltpu.VMEM(blocks, bf16),
            pltpu.VMEM((GROUPS, Y, 2, ROWS, WIDE), bf16),
            pltpu.VMEM((GROUPS, Y, 2, ROWS, FF), bf16),
            pltpu.VMEM(blocks, bf16),
            pltpu.VMEM(blocks, bf16),
            pltpu.VMEM((STEPS, 2, QROWS, HD), bf16),
            pltpu.VMEM((QROWS, HEADS * HD), bf16),
            pltpu.VMEM((TP * WIDE, 2 * FF), bf16),
            pltpu.VMEM((TP * FF, WIDE), bf16),
            pltpu.VMEM((GROUPS, FLAT, COLS * TOK), bf16),
            pltpu.VMEM((GROUPS, COLS * TOK, FLAT), bf16),
            pltpu.VMEM((GROUPS, COLS * TOK, FLAT), bf16),
            pltpu.VMEM((FLAT, FLAT), bf16),
            pltpu.VMEM((FLAT, FLAT), bf16),
            pltpu.VMEM((COLS * TOK, LANES), f32),
            dma((4,)),
            dma((GROUPS,)),
            dma((GROUPS,)),
            dma((GROUPS,)),
            dma((GROUPS,)),
            dma((GROUPS, 5)),
            dma((GROUPS, 5)),
            dma((GROUPS, 5)),
            dma((GROUPS, 5)),
            dma((STEPS + 1,)),
            dma((STEPS,)),
            pltpu.SemaphoreType.REGULAR,
        ],
        compiler_params=pltpu.CompilerParams(
            collective_id=0, has_side_effects=True, vmem_limit_bytes=60 * 1024 * 1024
        ),
    )(queries, keys_values, block_order, tokens, route_ids.T, route_gates.T, w_gate, w_up, w_down)


def solution(mesh):
    in_specs = (
        P("ctx", "tp"),
        P("ctx", "tp"),
        P(),
        P("ctx", "tp"),
        P("ctx", None),
        P("ctx", None),
        P("ctx", None, "tp"),
        P("ctx", None, "tp"),
        P("ctx", None, "tp"),
    )
    out_specs = (P("ctx", "tp"), P("ctx", "tp"))
    return jax.shard_map(shards, mesh=mesh, in_specs=in_specs, out_specs=out_specs, check_vma=False)
```

```python
import math

import jax
import jax.numpy as jnp
from jax import lax
from jax.experimental import pallas as pl
from jax.experimental.pallas import tpu as pltpu
from jax.sharding import PartitionSpec as P

HD = 128
EXPERTS = 64
TOPK = 8
STEPS = 4
CAP = 9
Z = 16
NEAR = 4
Y = 4
TP = 8
TOK = 64
QROWS = 128
HEADS = 8
WIDE = 512
LANES = 128
COLS = WIDE // LANES
HALF = Y * WIDE
FF = 128

OFFSETS = (1, 15, 3, 13, 4, 12, 7, 9, 0, 8, 6, 10, 5, 11, 2, 14)
PAIR = 2
GROUPS = 8
PER = PAIR * NEAR
ROWS = PER * CAP
FLAT = ROWS * COLS

MASKED = -1e30
f32 = jnp.float32
bf16 = jnp.bfloat16
i32 = jnp.int32


def dot(a, b):
    return jnp.dot(a, b, preferred_element_type=f32)


def iota(shape, dim):
    return lax.broadcasted_iota(i32, shape, dim)


def kernel(
    queries, keys_values, block_order, tokens, ids, gates, w_gate, w_up, w_down,
    attended, mixed,
    outgoing, arriving, rows_all, sums_here, sums_out, sums_in, hidden_all, going_back, returned, kv_all, q_here,
    w_in, w_out,
    dispatch, gate_high, gate_low, perm_in, perm_out, total,
    load_sem, w_send, w_recv, out_send, out_recv, back_send, back_recv, row_send, row_recv, sum_send, sum_recv,
    hid_send, hid_recv,
    kv_send, kv_recv, round_sem,
):
    ctx = lax.axis_index("ctx")
    tp = lax.axis_index("tp")
    n_ctx = Z * NEAR
    z, near = ctx // NEAR, ctx % NEAR
    x_lo, y = tp // Y, tp % Y
    barrier = pltpu.get_barrier_semaphore()

    def at(c, t):
        return {"ctx": c, "tp": t}

    def greet(c, t):
        pl.semaphore_signal(barrier, inc=1, device_id=at(c, t), device_id_type=pl.DeviceIdType.MESH)

    def send(src, dst, send_sem, recv_sem, c, t):
        copy = pltpu.make_async_remote_copy(
            src_ref=src, dst_ref=dst, send_sem=send_sem, recv_sem=recv_sem,
            device_id=at(c, t), device_id_type=pl.DeviceIdType.MESH,
        )
        copy.start()

    def wait(ref, sem):
        pltpu.make_async_copy(ref, ref, sem).wait()

    partner = (1 - x_lo) * Y + y

    for i in range(1, TP):
        greet(ctx, (tp + i) % TP)
    for i in range(1, NEAR):
        greet(z * NEAR + (near + i) % NEAR, tp)
    for i in (1, Z - 1):
        greet((z + i) % Z * NEAR + near, tp)

    def tell_z(i, steps):
        for way in (steps, Z - steps):
            pl.semaphore_signal(
                round_sem.at[i], inc=1, device_id=at((z + way) % Z * NEAR + near, tp),
                device_id_type=pl.DeviceIdType.MESH,
            )

    def tell_near(i):
        for d in range(1, NEAR):
            pl.semaphore_signal(
                round_sem.at[i], inc=1, device_id=at(z * NEAR + (near + d) % NEAR, tp),
                device_id_type=pl.DeviceIdType.MESH,
            )

    loads = [
        pltpu.make_async_copy(w_gate.at[0, pl.ds(x_lo * HALF, HALF)], w_in.at[:, pl.ds(0, FF)], load_sem.at[0]),
        pltpu.make_async_copy(w_up.at[0, pl.ds(x_lo * HALF, HALF)], w_in.at[:, pl.ds(FF, FF)], load_sem.at[1]),
        pltpu.make_async_copy(w_down.at[0], w_out, load_sem.at[2]),
        pltpu.make_async_copy(queries, q_here, load_sem.at[3]),
    ]
    for load in loads:
        load.start()

    place = iota((EXPERTS, TOK), 0)
    turn = lax.shift_right_logical(place, 2)
    offset = jnp.zeros((EXPERTS, TOK), i32)
    for i, o in enumerate(OFFSETS):
        offset = jnp.where(turn == i, o, offset)
    expert = ((z + offset) & (Z - 1)) * NEAR + (place & (NEAR - 1))
    named = jnp.zeros((EXPERTS, TOK), f32)
    gate_of = jnp.zeros((EXPERTS, TOK), f32)
    for k in range(TOPK):
        hit = ids[pl.ds(k, 1), :] == expert
        named = jnp.where(hit, 1.0, named)
        gate_of = jnp.where(hit, gates[pl.ds(k, 1), :], gate_of)
    earlier = (iota((TOK, TOK), 0) < iota((TOK, TOK), 1)).astype(f32).astype(bf16)
    rank = dot(named.astype(bf16), earlier)
    coded = jnp.concatenate(
        [jnp.where(named > 0, rank + 16.0 * j, -1.0) for j in range(COLS)], axis=1
    ).astype(bf16)
    gate4 = jnp.concatenate([gate_of] * COLS, axis=1)
    gate4_high = gate4.astype(bf16)
    gate4_low = (gate4 - gate4_high.astype(f32)).astype(bf16)

    line = iota((FLAT, LANES), 0).astype(f32)
    block = jnp.floor((line + 0.5) * (1.0 / (CAP * COLS)))
    within = line - block * (CAP * COLS)
    slot = jnp.floor((within + 0.5) * (1.0 / COLS))
    code = slot + 16.0 * (within - slot * COLS)
    spread = (block[:, :PER] == iota((FLAT, PER), 1).astype(f32)).astype(f32).astype(bf16)
    token_cols = jnp.concatenate(
        [tokens[:, pl.ds(j * LANES, LANES)] for j in range(COLS)], axis=0
    )

    def fill(g):
        codes = dot(spread, coded[g * PER:(g + 1) * PER])
        chosen = jnp.concatenate(
            [(codes[:, :LANES] == code).astype(f32), (codes[:, LANES:] == code).astype(f32)], axis=1
        ).astype(bf16)
        dispatch[g] = chosen
        outgoing[pl.ds(g * PER, PER)] = (
            dot(chosen, token_cols).astype(bf16).reshape(PER, CAP, COLS, LANES)
        )

    for g in range(GROUPS):
        fill(g)

    to = iota((FLAT, FLAT), 1).astype(f32)
    at_row = iota((FLAT, FLAT), 0).astype(f32)
    col = jnp.floor((at_row + 0.5) * (1.0 / ROWS))
    perm_in[...] = (to == COLS * (at_row - ROWS * col) + col).astype(f32).astype(bf16)
    row = jnp.floor((at_row + 0.5) * (1.0 / COLS))
    perm_out[...] = (to == ROWS * (at_row - COLS * row) + row).astype(f32).astype(bf16)

    pl.semaphore_wait(barrier, (TP - 1) + (NEAR - 1) + 2)
    tell_z(0, 1)
    tell_near(0)

    def send_block(src, dst, send_sems, recv_sems, p, d, way):
        g, o, base = p // PAIR, OFFSETS[p], p * NEAR
        there = (near + d) % NEAR
        if o == 0 and d == 0:
            pltpu.make_async_copy(src.at[base + near], dst.at[base + near], recv_sems.at[g]).start()
        else:
            send(
                src.at[base + there], dst.at[base + near], send_sems.at[g], recv_sems.at[g],
                (z + way * o + Z) % Z * NEAR + there, tp,
            )

    def dispatch_to(offsets, places):
        for o in offsets:
            for d in places:
                send_block(outgoing, arriving, out_send, out_recv, OFFSETS.index(o), d, 1)

    same, others, every = (0,), (1, 2, 3), (0, 1, 2, 3)
    dispatch_to((1, 15), same)
    dispatch_to((0,), every)
    theirs = pl.ds((1 - x_lo) * HALF, HALF)
    send(w_gate.at[0, theirs], w_in.at[:, pl.ds(2 * FF, FF)], w_send.at[0], w_recv.at[0], ctx, partner)
    send(w_up.at[0, theirs], w_in.at[:, pl.ds(3 * FF, FF)], w_send.at[1], w_recv.at[1], ctx, partner)

    for d in range(2):
        target = 2 * (tp % 4) + d
        dst = kv_all.at[0, tp // 4]

        @pl.when(target != tp)
        def _():
            send(keys_values, dst, kv_send.at[d], kv_recv.at[0], ctx, target)

        @pl.when(target == tp)
        def _():
            pltpu.make_async_copy(keys_values, dst, kv_recv.at[0]).start()

    pl.semaphore_wait(round_sem.at[0], 2 + NEAR - 1)
    tell_z(1, 2)
    dispatch_to((1, 15), others)
    pl.semaphore_wait(round_sem.at[1], 2)
    tell_z(2, 4)
    dispatch_to((3, 13), every)
    dispatch_to((4, 12), same)
    pl.semaphore_wait(round_sem.at[2], 2)
    tell_near(3)
    dispatch_to((4, 12), others)
    dispatch_to((7, 9), every)
    dispatch_to((8,), same)
    pl.semaphore_wait(round_sem.at[3], NEAR - 1)
    dispatch_to((8,), others)
    dispatch_to((6, 10, 5, 11, 2, 14), every)

    def pass_kv(s):
        wait(kv_all.at[s - 1], kv_recv.at[s - 1])
        send(kv_all.at[s - 1], kv_all.at[s], kv_send.at[s + 1], kv_recv.at[s], (ctx + 1) % n_ctx, tp)

    for g in range(GROUPS):
        high = dot(spread, gate4_high[g * PER:(g + 1) * PER])
        low = dot(spread, gate4_low[g * PER:(g + 1) * PER])
        chosen = dispatch[g].astype(f32)
        gate_high[g] = (chosen * high).T.astype(bf16)
        gate_low[g] = (chosen * low).T.astype(bf16)

    def take_rows(g):
        wait(arriving.at[pl.ds(g * PER, PER)], out_recv.at[g])
        flat = arriving[pl.ds(g * PER, PER)].reshape(FLAT, LANES)
        sorted_rows = dot(perm_in[...], flat)
        for j in range(COLS):
            rows_all[g, y, :, pl.ds(j * LANES, LANES)] = sorted_rows[j * ROWS:(j + 1) * ROWS].astype(bf16)
        mine = rows_all.at[g, y]
        for i in (2, 1, 3):
            send(mine, mine, row_send.at[g], row_recv.at[g], ctx, x_lo * Y + (y + i) % Y)

    def first_half(g):
        if g == 0:
            loads[0].wait()
            loads[1].wait()
            for i in range(2):
                wait(w_in.at[:, pl.ds((2 + i) * FF, FF)], w_recv.at[i])
        wait(rows_all.at[g, pl.ds(0, Y - 1)], row_recv.at[g])
        sums = jnp.zeros((ROWS, 4 * FF), f32)
        for yy in range(Y):
            sums += dot(rows_all[g, yy], w_in[pl.ds(yy * WIDE, WIDE), :])
        sums_out[g] = sums[:, 2 * FF:]
        sums_here[g] = sums[:, :2 * FF]
        send(sums_out.at[g], sums_in.at[g], sum_send.at[g], sum_recv.at[g], ctx, partner)

    def activate(g):
        wait(sums_in.at[g], sum_recv.at[g])
        sums = sums_here[g] + sums_in[g]
        gate_sum, up_sum = sums[:, :FF], sums[:, FF:]
        hidden = gate_sum / (1.0 + jnp.exp(-gate_sum)) * up_sum
        hidden_all[g, tp] = hidden.astype(bf16)
        mine = hidden_all.at[g, tp]
        for i in (6, 2, 5, 7, 1, 3, 4):
            send(mine, mine, hid_send.at[g], hid_recv.at[g], ctx, (tp + i) % TP)

    def second_half(g):
        if g == 0:
            loads[2].wait()
        wait(hidden_all.at[g, pl.ds(0, TP - 1)], hid_recv.at[g])
        sums = jnp.zeros((ROWS, WIDE), f32)
        for t in range(TP):
            sums += dot(hidden_all[g, t], w_out[pl.ds(t * FF, FF), :])
        stacked = jnp.concatenate(
            [sums[:, j * LANES:(j + 1) * LANES] for j in range(COLS)], axis=0
        ).astype(bf16)
        going_back[pl.ds(g * PER, PER)] = (
            dot(perm_out[...], stacked).astype(bf16).reshape(PER, CAP, COLS, LANES)
        )
        for p in range(g * PAIR, (g + 1) * PAIR):
            for d in range(NEAR):
                send_block(going_back, returned, back_send, back_recv, p, d, -1)

    def mix(g):
        wait(returned.at[pl.ds(g * PER, PER)], back_recv.at[g])
        flat = returned[pl.ds(g * PER, PER)].reshape(FLAT, LANES)
        part = dot(gate_high[g], flat) + dot(gate_low[g], flat)
        if g == 0:
            total[...] = part
        else:
            total[...] += part

    own_block = block_order[ctx]

    def attend(first, last):
        if first == 0:
            loads[3].wait()
            wait(kv_all.at[STEPS - 1], kv_recv.at[STEPS - 1])
        query_place = own_block * QROWS + iota((QROWS, QROWS), 0)
        key_offset = iota((QROWS, QROWS), 1)
        visible = jnp.concatenate(
            [
                jnp.where(
                    block_order[(ctx + n_ctx - s) % n_ctx] * QROWS + key_offset <= query_place, 1.0, 0.0
                )
                for s in range(STEPS)
            ],
            axis=1,
        )
        keys = jnp.concatenate([kv_all[s, 0] for s in range(STEPS)], axis=0)
        values = jnp.concatenate([kv_all[s, 1] for s in range(STEPS)], axis=0)
        for h in range(first, last):
            scores = lax.dot_general(
                q_here[:, pl.ds(h * HD, HD)], keys, (((1,), (1,)), ((), ())),
                preferred_element_type=f32,
            ) * (1.0 / math.sqrt(HD))
            scores = jnp.where(visible > 0.5, scores, MASKED)
            weights = jnp.exp(scores - jnp.max(scores, axis=1, keepdims=True))
            weight_total = jnp.sum(weights, axis=1, keepdims=True)
            blended = dot(weights.astype(bf16), values) / weight_total
            attended[:, pl.ds(h * HD, HD)] = blended.astype(bf16)

    take_rows(0)
    take_rows(1)
    take_rows(2)
    take_rows(3)
    first_half(0)
    first_half(1)
    first_half(2)
    activate(0)
    activate(1)
    take_rows(4)
    first_half(3)
    activate(2)
    second_half(0)
    second_half(1)
    pass_kv(1)
    take_rows(5)
    first_half(4)
    activate(3)
    second_half(2)
    take_rows(6)
    first_half(5)
    activate(4)
    second_half(3)
    pass_kv(2)
    take_rows(7)
    first_half(6)
    activate(5)
    second_half(4)
    first_half(7)
    activate(6)
    second_half(5)
    pass_kv(3)
    activate(7)
    second_half(6)
    second_half(7)
    attend(0, 8)
    mix(0)
    mix(1)
    mix(2)
    mix(3)
    mix(4)
    mix(5)
    mix(6)
    mix(7)
    for j in range(COLS):
        mixed[:, pl.ds(j * LANES, LANES)] = total[pl.ds(j * TOK, TOK), :].astype(bf16)

    for g in range(GROUPS):
        count = PER - 1 if 0 in OFFSETS[g * PAIR:(g + 1) * PAIR] else PER
        wait(outgoing.at[pl.ds(g * PER, count)], out_send.at[g])
        wait(going_back.at[pl.ds(g * PER, count)], back_send.at[g])
        wait(rows_all.at[g, pl.ds(0, Y - 1)], row_send.at[g])
        wait(sums_out.at[g], sum_send.at[g])
        wait(hidden_all.at[g, pl.ds(0, TP - 1)], hid_send.at[g])
    for i in range(2):
        wait(w_in.at[:, pl.ds((2 + i) * FF, FF)], w_send.at[i])
    for d in range(2):
        @pl.when(2 * (tp % 4) + d != tp)
        def _():
            wait(keys_values, kv_send.at[d])
    for s in range(1, STEPS):
        wait(kv_all.at[s], kv_send.at[s + 1])


def shards(queries, keys_values, block_order, tokens, route_ids, route_gates, w_gate, w_up, w_down):
    vmem = pl.BlockSpec(memory_space=pltpu.VMEM)
    smem = pl.BlockSpec(memory_space=pltpu.SMEM)
    anywhere = pl.BlockSpec(memory_space=pl.ANY)
    dma = pltpu.SemaphoreType.DMA
    blocks = (GROUPS * PER, CAP, COLS, LANES)
    return pl.pallas_call(
        kernel,
        out_shape=(
            jax.ShapeDtypeStruct((QROWS, HEADS * HD), bf16),
            jax.ShapeDtypeStruct((TOK, WIDE), bf16),
        ),
        in_specs=[anywhere, vmem, smem, vmem, vmem, vmem, anywhere, anywhere, anywhere],
        out_specs=(vmem, vmem),
        scratch_shapes=[
            pltpu.VMEM(blocks, bf16),
            pltpu.VMEM(blocks, bf16),
            pltpu.VMEM((GROUPS, Y, ROWS, WIDE), bf16),
            pltpu.VMEM((GROUPS, ROWS, 2 * FF), f32),
            pltpu.VMEM((GROUPS, ROWS, 2 * FF), f32),
            pltpu.VMEM((GROUPS, ROWS, 2 * FF), f32),
            pltpu.VMEM((GROUPS, TP, ROWS, FF), bf16),
            pltpu.VMEM(blocks, bf16),
            pltpu.VMEM(blocks, bf16),
            pltpu.VMEM((STEPS, 2, QROWS, HD), bf16),
            pltpu.VMEM((QROWS, HEADS * HD), bf16),
            pltpu.VMEM((HALF, 4 * FF), bf16),
            pltpu.VMEM((TP * FF, WIDE), bf16),
            pltpu.VMEM((GROUPS, FLAT, COLS * TOK), bf16),
            pltpu.VMEM((GROUPS, COLS * TOK, FLAT), bf16),
            pltpu.VMEM((GROUPS, COLS * TOK, FLAT), bf16),
            pltpu.VMEM((FLAT, FLAT), bf16),
            pltpu.VMEM((FLAT, FLAT), bf16),
            pltpu.VMEM((COLS * TOK, LANES), f32),
            dma((4,)),
            dma((2,)),
            dma((2,)),
            dma((GROUPS,)),
            dma((GROUPS,)),
            dma((GROUPS,)),
            dma((GROUPS,)),
            dma((GROUPS,)),
            dma((GROUPS,)),
            dma((GROUPS,)),
            dma((GROUPS,)),
            dma((GROUPS,)),
            dma((GROUPS,)),
            dma((STEPS + 1,)),
            dma((STEPS,)),
            pltpu.SemaphoreType.REGULAR((4,)),
        ],
        compiler_params=pltpu.CompilerParams(
            collective_id=0, has_side_effects=True, vmem_limit_bytes=60 * 1024 * 1024
        ),
    )(queries, keys_values, block_order, tokens, route_ids.T, route_gates.T, w_gate, w_up, w_down)


def solution(mesh):
    in_specs = (
        P("ctx", "tp"),
        P("ctx", "tp"),
        P(),
        P("ctx", "tp"),
        P("ctx", None),
        P("ctx", None),
        P("ctx", None, "tp"),
        P("ctx", None, "tp"),
        P("ctx", None, "tp"),
    )
    out_specs = (P("ctx", "tp"), P("ctx", "tp"))
    return jax.shard_map(shards, mesh=mesh, in_specs=in_specs, out_specs=out_specs, check_vma=False)
```

```python
import math

import jax
import jax.numpy as jnp
from jax import lax
from jax.experimental import pallas as pl
from jax.experimental.pallas import tpu as pltpu
from jax.sharding import PartitionSpec as P

HD = 128
EXPERTS = 64
TOPK = 8
STEPS = 4
CAP = 9
Z = 16
NEAR = 4
Y = 4
TP = 8
TOK = 64
QROWS = 128
HEADS = 8
WIDE = 512
LANES = 128
COLS = WIDE // LANES
HALF = Y * WIDE
FF = 128

OFFSETS = (1, 15, 3, 13, 4, 12, 7, 9, 0, 8, 6, 10, 5, 11, 2, 14)
PAIR = 2
GROUPS = 8
PER = PAIR * NEAR
ROWS = PER * CAP
FLAT = ROWS * COLS

MASKED = -1e30
f32 = jnp.float32
bf16 = jnp.bfloat16
i32 = jnp.int32


def dot(a, b):
    return jnp.dot(a, b, preferred_element_type=f32)


def iota(shape, dim):
    return lax.broadcasted_iota(i32, shape, dim)


def kernel(
    queries, keys_values, block_order, tokens, ids, gates, w_gate, w_up, w_down,
    attended, mixed,
    outgoing, arriving, rows_all, sums_here, sums_out, sums_in, hidden_all, going_back, returned, kv_all, q_here,
    w_in, w_out,
    dispatch, gate_high, gate_low, perm_in, perm_out, total,
    load_sem, w_send, w_recv, out_send, out_recv, back_send, back_recv, row_send, row_recv, sum_send, sum_recv,
    hid_send, hid_recv,
    kv_send, kv_recv, round_sem,
):
    ctx = lax.axis_index("ctx")
    tp = lax.axis_index("tp")
    n_ctx = Z * NEAR
    z, near = ctx // NEAR, ctx % NEAR
    x_lo, y = tp // Y, tp % Y
    barrier = pltpu.get_barrier_semaphore()

    def at(c, t):
        return {"ctx": c, "tp": t}

    def greet(c, t):
        pl.semaphore_signal(barrier, inc=1, device_id=at(c, t), device_id_type=pl.DeviceIdType.MESH)

    def send(src, dst, send_sem, recv_sem, c, t):
        copy = pltpu.make_async_remote_copy(
            src_ref=src, dst_ref=dst, send_sem=send_sem, recv_sem=recv_sem,
            device_id=at(c, t), device_id_type=pl.DeviceIdType.MESH,
        )
        copy.start()

    def wait(ref, sem):
        pltpu.make_async_copy(ref, ref, sem).wait()

    partner = (1 - x_lo) * Y + y

    for i in range(1, TP):
        greet(ctx, (tp + i) % TP)
    for i in range(1, NEAR):
        greet(z * NEAR + (near + i) % NEAR, tp)
    for i in (1, Z - 1):
        greet((z + i) % Z * NEAR + near, tp)

    def tell_z(i, steps):
        for way in (steps, Z - steps):
            pl.semaphore_signal(
                round_sem.at[i], inc=1, device_id=at((z + way) % Z * NEAR + near, tp),
                device_id_type=pl.DeviceIdType.MESH,
            )

    def tell_near(i):
        for d in range(1, NEAR):
            pl.semaphore_signal(
                round_sem.at[i], inc=1, device_id=at(z * NEAR + (near + d) % NEAR, tp),
                device_id_type=pl.DeviceIdType.MESH,
            )

    loads = [
        pltpu.make_async_copy(w_gate.at[0, pl.ds(x_lo * HALF, HALF)], w_in.at[:, pl.ds(0, FF)], load_sem.at[0]),
        pltpu.make_async_copy(w_up.at[0, pl.ds(x_lo * HALF, HALF)], w_in.at[:, pl.ds(FF, FF)], load_sem.at[1]),
        pltpu.make_async_copy(w_down.at[0], w_out, load_sem.at[2]),
        pltpu.make_async_copy(queries, q_here, load_sem.at[3]),
    ]
    for load in loads:
        load.start()

    place = iota((EXPERTS, TOK), 0)
    turn = lax.shift_right_logical(place, 2)
    offset = jnp.zeros((EXPERTS, TOK), i32)
    for i, o in enumerate(OFFSETS):
        offset = jnp.where(turn == i, o, offset)
    expert = ((z + offset) & (Z - 1)) * NEAR + (place & (NEAR - 1))
    named = jnp.zeros((EXPERTS, TOK), f32)
    gate_of = jnp.zeros((EXPERTS, TOK), f32)
    for k in range(TOPK):
        hit = ids[pl.ds(k, 1), :] == expert
        named = jnp.where(hit, 1.0, named)
        gate_of = jnp.where(hit, gates[pl.ds(k, 1), :], gate_of)
    earlier = (iota((TOK, TOK), 0) < iota((TOK, TOK), 1)).astype(f32).astype(bf16)
    rank = dot(named.astype(bf16), earlier)
    coded = jnp.concatenate(
        [jnp.where(named > 0, rank + 16.0 * j, -1.0) for j in range(COLS)], axis=1
    ).astype(bf16)
    gate4 = jnp.concatenate([gate_of] * COLS, axis=1)
    gate4_high = gate4.astype(bf16)
    gate4_low = (gate4 - gate4_high.astype(f32)).astype(bf16)

    line = iota((FLAT, LANES), 0).astype(f32)
    block = jnp.floor((line + 0.5) * (1.0 / (CAP * COLS)))
    within = line - block * (CAP * COLS)
    slot = jnp.floor((within + 0.5) * (1.0 / COLS))
    code = slot + 16.0 * (within - slot * COLS)
    spread = (block[:, :PER] == iota((FLAT, PER), 1).astype(f32)).astype(f32).astype(bf16)
    token_cols = jnp.concatenate(
        [tokens[:, pl.ds(j * LANES, LANES)] for j in range(COLS)], axis=0
    )

    def fill(g):
        codes = dot(spread, coded[g * PER:(g + 1) * PER])
        chosen = jnp.concatenate(
            [(codes[:, :LANES] == code).astype(f32), (codes[:, LANES:] == code).astype(f32)], axis=1
        ).astype(bf16)
        dispatch[g] = chosen
        outgoing[pl.ds(g * PER, PER)] = (
            dot(chosen, token_cols).astype(bf16).reshape(PER, CAP, COLS, LANES)
        )

    for g in range(GROUPS):
        fill(g)

    to = iota((FLAT, FLAT), 1).astype(f32)
    at_row = iota((FLAT, FLAT), 0).astype(f32)
    col = jnp.floor((at_row + 0.5) * (1.0 / ROWS))
    perm_in[...] = (to == COLS * (at_row - ROWS * col) + col).astype(f32).astype(bf16)
    row = jnp.floor((at_row + 0.5) * (1.0 / COLS))
    perm_out[...] = (to == ROWS * (at_row - COLS * row) + row).astype(f32).astype(bf16)

    pl.semaphore_wait(barrier, (TP - 1) + (NEAR - 1) + 2)
    tell_z(0, 1)
    tell_near(0)

    def send_block(src, dst, send_sems, recv_sems, p, d, way):
        g, o, base = p // PAIR, OFFSETS[p], p * NEAR
        there = (near + d) % NEAR
        if o == 0 and d == 0:
            pltpu.make_async_copy(src.at[base + near], dst.at[base + near], recv_sems.at[g]).start()
        else:
            send(
                src.at[base + there], dst.at[base + near], send_sems.at[g], recv_sems.at[g],
                (z + way * o + Z) % Z * NEAR + there, tp,
            )

    def dispatch_to(offsets, places):
        for o in offsets:
            for d in places:
                send_block(outgoing, arriving, out_send, out_recv, OFFSETS.index(o), d, 1)

    same, others, every = (0,), (1, 2, 3), (0, 1, 2, 3)
    dispatch_to((1, 15), same)
    dispatch_to((0,), every)
    theirs = pl.ds((1 - x_lo) * HALF, HALF)
    send(w_gate.at[0, theirs], w_in.at[:, pl.ds(2 * FF, FF)], w_send.at[0], w_recv.at[0], ctx, partner)
    send(w_up.at[0, theirs], w_in.at[:, pl.ds(3 * FF, FF)], w_send.at[1], w_recv.at[1], ctx, partner)

    for d in range(2):
        target = 2 * (tp % 4) + d
        dst = kv_all.at[0, tp // 4]

        @pl.when(target != tp)
        def _():
            send(keys_values, dst, kv_send.at[d], kv_recv.at[0], ctx, target)

        @pl.when(target == tp)
        def _():
            pltpu.make_async_copy(keys_values, dst, kv_recv.at[0]).start()

    pl.semaphore_wait(round_sem.at[0], 2 + NEAR - 1)
    tell_z(1, 2)
    dispatch_to((1, 15), others)
    pl.semaphore_wait(round_sem.at[1], 2)
    tell_z(2, 4)
    dispatch_to((3, 13), every)
    dispatch_to((4, 12), same)
    pl.semaphore_wait(round_sem.at[2], 2)
    tell_near(3)
    dispatch_to((4, 12), others)
    dispatch_to((7, 9), every)
    dispatch_to((8,), same)
    pl.semaphore_wait(round_sem.at[3], NEAR - 1)
    dispatch_to((8,), others)
    dispatch_to((6, 10, 5, 11, 2, 14), every)

    def pass_kv(s):
        wait(kv_all.at[s - 1], kv_recv.at[s - 1])
        send(kv_all.at[s - 1], kv_all.at[s], kv_send.at[s + 1], kv_recv.at[s], (ctx + 1) % n_ctx, tp)

    for g in range(GROUPS):
        high = dot(spread, gate4_high[g * PER:(g + 1) * PER])
        low = dot(spread, gate4_low[g * PER:(g + 1) * PER])
        chosen = dispatch[g].astype(f32)
        gate_high[g] = (chosen * high).T.astype(bf16)
        gate_low[g] = (chosen * low).T.astype(bf16)

    def take_rows(g):
        wait(arriving.at[pl.ds(g * PER, PER)], out_recv.at[g])
        flat = arriving[pl.ds(g * PER, PER)].reshape(FLAT, LANES)
        sorted_rows = dot(perm_in[...], flat)
        for j in range(COLS):
            rows_all[g, y, :, pl.ds(j * LANES, LANES)] = sorted_rows[j * ROWS:(j + 1) * ROWS].astype(bf16)
        mine = rows_all.at[g, y]
        for i in (2, 1, 3):
            send(mine, mine, row_send.at[g], row_recv.at[g], ctx, x_lo * Y + (y + i) % Y)

    def first_half(g):
        if g == 0:
            loads[0].wait()
            loads[1].wait()
            for i in range(2):
                wait(w_in.at[:, pl.ds((2 + i) * FF, FF)], w_recv.at[i])
        wait(rows_all.at[g, pl.ds(0, Y - 1)], row_recv.at[g])
        sums = jnp.zeros((ROWS, 4 * FF), f32)
        for yy in range(Y):
            sums += dot(rows_all[g, yy], w_in[pl.ds(yy * WIDE, WIDE), :])
        sums_out[g] = sums[:, 2 * FF:]
        sums_here[g] = sums[:, :2 * FF]
        send(sums_out.at[g], sums_in.at[g], sum_send.at[g], sum_recv.at[g], ctx, partner)

    def activate(g):
        wait(sums_in.at[g], sum_recv.at[g])
        sums = sums_here[g] + sums_in[g]
        gate_sum, up_sum = sums[:, :FF], sums[:, FF:]
        hidden = gate_sum / (1.0 + jnp.exp(-gate_sum)) * up_sum
        hidden_all[g, tp] = hidden.astype(bf16)
        mine = hidden_all.at[g, tp]
        for i in (6, 2, 5, 7, 1, 3, 4):
            send(mine, mine, hid_send.at[g], hid_recv.at[g], ctx, (tp + i) % TP)

    def second_half(g):
        if g == 0:
            loads[2].wait()
        wait(hidden_all.at[g, pl.ds(0, TP - 1)], hid_recv.at[g])
        sums = jnp.zeros((ROWS, WIDE), f32)
        for t in range(TP):
            sums += dot(hidden_all[g, t], w_out[pl.ds(t * FF, FF), :])
        stacked = jnp.concatenate(
            [sums[:, j * LANES:(j + 1) * LANES] for j in range(COLS)], axis=0
        ).astype(bf16)
        going_back[pl.ds(g * PER, PER)] = (
            dot(perm_out[...], stacked).astype(bf16).reshape(PER, CAP, COLS, LANES)
        )
        for p in range(g * PAIR, (g + 1) * PAIR):
            for d in range(NEAR):
                send_block(going_back, returned, back_send, back_recv, p, d, -1)

    def mix(g):
        wait(returned.at[pl.ds(g * PER, PER)], back_recv.at[g])
        flat = returned[pl.ds(g * PER, PER)].reshape(FLAT, LANES)
        part = dot(gate_high[g], flat) + dot(gate_low[g], flat)
        if g == 0:
            total[...] = part
        else:
            total[...] += part

    own_block = block_order[ctx]

    def attend(first, last):
        if first == 0:
            loads[3].wait()
            wait(kv_all.at[STEPS - 1], kv_recv.at[STEPS - 1])
        query_place = own_block * QROWS + iota((QROWS, QROWS), 0)
        key_offset = iota((QROWS, QROWS), 1)
        visible = jnp.concatenate(
            [
                jnp.where(
                    block_order[(ctx + n_ctx - s) % n_ctx] * QROWS + key_offset <= query_place, 1.0, 0.0
                )
                for s in range(STEPS)
            ],
            axis=1,
        )
        keys = jnp.concatenate([kv_all[s, 0] for s in range(STEPS)], axis=0)
        values = jnp.concatenate([kv_all[s, 1] for s in range(STEPS)], axis=0)
        for h in range(first, last):
            scores = lax.dot_general(
                q_here[:, pl.ds(h * HD, HD)], keys, (((1,), (1,)), ((), ())),
                preferred_element_type=f32,
            ) * (1.0 / math.sqrt(HD))
            scores = jnp.where(visible > 0.5, scores, MASKED)
            weights = jnp.exp(scores - jnp.max(scores, axis=1, keepdims=True))
            weight_total = jnp.sum(weights, axis=1, keepdims=True)
            blended = dot(weights.astype(bf16), values) / weight_total
            attended[:, pl.ds(h * HD, HD)] = blended.astype(bf16)

    take_rows(0)
    take_rows(1)
    take_rows(2)
    take_rows(3)
    first_half(0)
    first_half(1)
    first_half(2)
    activate(0)
    activate(1)
    take_rows(4)
    first_half(3)
    activate(2)
    second_half(0)
    second_half(1)
    pass_kv(1)
    take_rows(5)
    first_half(4)
    activate(3)
    second_half(2)
    take_rows(6)
    first_half(5)
    activate(4)
    second_half(3)
    pass_kv(2)
    take_rows(7)
    first_half(6)
    activate(5)
    second_half(4)
    pass_kv(3)
    first_half(7)
    activate(6)
    second_half(5)
    activate(7)
    attend(0, 4)
    second_half(6)
    attend(4, 8)
    second_half(7)
    mix(0)
    mix(1)
    mix(2)
    mix(3)
    mix(4)
    mix(5)
    mix(6)
    mix(7)
    for j in range(COLS):
        mixed[:, pl.ds(j * LANES, LANES)] = total[pl.ds(j * TOK, TOK), :].astype(bf16)

    for g in range(GROUPS):
        count = PER - 1 if 0 in OFFSETS[g * PAIR:(g + 1) * PAIR] else PER
        wait(outgoing.at[pl.ds(g * PER, count)], out_send.at[g])
        wait(going_back.at[pl.ds(g * PER, count)], back_send.at[g])
        wait(rows_all.at[g, pl.ds(0, Y - 1)], row_send.at[g])
        wait(sums_out.at[g], sum_send.at[g])
        wait(hidden_all.at[g, pl.ds(0, TP - 1)], hid_send.at[g])
    for i in range(2):
        wait(w_in.at[:, pl.ds((2 + i) * FF, FF)], w_send.at[i])
    for d in range(2):
        @pl.when(2 * (tp % 4) + d != tp)
        def _():
            wait(keys_values, kv_send.at[d])
    for s in range(1, STEPS):
        wait(kv_all.at[s], kv_send.at[s + 1])


def shards(queries, keys_values, block_order, tokens, route_ids, route_gates, w_gate, w_up, w_down):
    vmem = pl.BlockSpec(memory_space=pltpu.VMEM)
    smem = pl.BlockSpec(memory_space=pltpu.SMEM)
    anywhere = pl.BlockSpec(memory_space=pl.ANY)
    dma = pltpu.SemaphoreType.DMA
    blocks = (GROUPS * PER, CAP, COLS, LANES)
    return pl.pallas_call(
        kernel,
        out_shape=(
            jax.ShapeDtypeStruct((QROWS, HEADS * HD), bf16),
            jax.ShapeDtypeStruct((TOK, WIDE), bf16),
        ),
        in_specs=[anywhere, vmem, smem, vmem, vmem, vmem, anywhere, anywhere, anywhere],
        out_specs=(vmem, vmem),
        scratch_shapes=[
            pltpu.VMEM(blocks, bf16),
            pltpu.VMEM(blocks, bf16),
            pltpu.VMEM((GROUPS, Y, ROWS, WIDE), bf16),
            pltpu.VMEM((GROUPS, ROWS, 2 * FF), f32),
            pltpu.VMEM((GROUPS, ROWS, 2 * FF), f32),
            pltpu.VMEM((GROUPS, ROWS, 2 * FF), f32),
            pltpu.VMEM((GROUPS, TP, ROWS, FF), bf16),
            pltpu.VMEM(blocks, bf16),
            pltpu.VMEM(blocks, bf16),
            pltpu.VMEM((STEPS, 2, QROWS, HD), bf16),
            pltpu.VMEM((QROWS, HEADS * HD), bf16),
            pltpu.VMEM((HALF, 4 * FF), bf16),
            pltpu.VMEM((TP * FF, WIDE), bf16),
            pltpu.VMEM((GROUPS, FLAT, COLS * TOK), bf16),
            pltpu.VMEM((GROUPS, COLS * TOK, FLAT), bf16),
            pltpu.VMEM((GROUPS, COLS * TOK, FLAT), bf16),
            pltpu.VMEM((FLAT, FLAT), bf16),
            pltpu.VMEM((FLAT, FLAT), bf16),
            pltpu.VMEM((COLS * TOK, LANES), f32),
            dma((4,)),
            dma((2,)),
            dma((2,)),
            dma((GROUPS,)),
            dma((GROUPS,)),
            dma((GROUPS,)),
            dma((GROUPS,)),
            dma((GROUPS,)),
            dma((GROUPS,)),
            dma((GROUPS,)),
            dma((GROUPS,)),
            dma((GROUPS,)),
            dma((GROUPS,)),
            dma((STEPS + 1,)),
            dma((STEPS,)),
            pltpu.SemaphoreType.REGULAR((4,)),
        ],
        compiler_params=pltpu.CompilerParams(
            collective_id=0, has_side_effects=True, vmem_limit_bytes=60 * 1024 * 1024
        ),
    )(queries, keys_values, block_order, tokens, route_ids.T, route_gates.T, w_gate, w_up, w_down)


def solution(mesh):
    in_specs = (
        P("ctx", "tp"),
        P("ctx", "tp"),
        P(),
        P("ctx", "tp"),
        P("ctx", None),
        P("ctx", None),
        P("ctx", None, "tp"),
        P("ctx", None, "tp"),
        P("ctx", None, "tp"),
    )
    out_specs = (P("ctx", "tp"), P("ctx", "tp"))
    return jax.shard_map(shards, mesh=mesh, in_specs=in_specs, out_specs=out_specs, check_vma=False)
```
